512 devices in a mesh: dp: 64 (over y, z), tensor: 8 (over x, core).
Axes of the slice: x: 4, y: 8, z: 8, core: 2. Of those that a mesh axis runs over, the one named last changes fastest.
Arguments:
- activations: bfloat16 [65536, 3072], P('dp', 'tensor'), may hold values from -6 to 6
- out_grads: bfloat16 [65536, 2560], P('dp'), may hold values from -0.25 to 0.25
- residue: bfloat16 [64, 3072, 2560], P('dp', 'tensor'), may hold values from -6 to 6
- warm_start: bfloat16 [2560, 64], replicated, may hold values from -6 to 6
Outputs:
- update: bfloat16 [3072, 2560], P('tensor')
The draws below stay inside these ranges and needn't reach their ends.
All inputs are finite; a program needn't handle non-finite values.
Results may differ from the reference program's by a relative error of at most 0.0011.
Values sent between devices are 32-bit elements; how exact they have to be, the bound alone decides.
No kernel may reach another device: no remote copies, remote signals or barrier semaphores. Data moves between devices by JAX's collectives and lax.ppermute only.
A program may use at most 64 MiB of HBM per device.

```python
import jax
import jax.numpy as jnp
from jax import lax

COLS = 2560
RANK = 64
TOK_DEV = 1024
ROWS = 3072
TOKENS = 65536
REPLICAS = 64
N_DP = 64


def block_levels(stream_key, shape, cuts, least, high):
    gain, own = 1.0, jax.random.fold_in(stream_key, 6)
    for dim, blocks in cuts:
        heights = jnp.exp(jax.random.uniform(jax.random.fold_in(own, dim), (blocks,), jnp.float32, least / len(cuts), high / len(cuts)))
        gain = gain * jnp.repeat(heights, shape[dim] // blocks).reshape([-1 if axis == dim else 1 for axis in range(len(shape))])
    return gain


def centred(own_key, extent, width, limit, shards=(), dtype=jnp.bfloat16):
    factor_of = block_levels(own_key, extent, shards, -0.22, 0.18) if shards else 1.0
    values = jax.random.normal(own_key, extent, jnp.float32) * width * factor_of
    return jnp.minimum(jnp.maximum(values, -limit), limit).astype(dtype)


def setup_inputs(seed: int = 0) -> dict:
    splits = jax.random.split(jax.random.key(seed), 5)
    return {
        "activations": centred(splits[0], (TOKENS, ROWS), 1.0, 6.0, ((0, 64), (1, 8))),
        "out_grads": centred(splits[1], (TOKENS, COLS), (0.5 / TOK_DEV ** 0.5), 0.25, ((0, 64),)),
        "residue": centred(splits[2], (REPLICAS, ROWS, COLS), 0.5, 6.0, ((0, 64), (1, 8))),
        "warm_start": centred(splits[3], (COLS, RANK), 1.0, 6.0),
    }


highest_precision = lax.Precision.HIGHEST

def whiten(lower_factor, matrix):
    return jax.scipy.linalg.solve_triangular(lower_factor, matrix.T, lower=True).T

def merged_of(tok_block, grad_block, error_block):
    gradient = jnp.dot(tok_block.T.astype(jnp.float32), grad_block.astype(jnp.float32), preferred_element_type=jnp.float32)
    return gradient + error_block.astype(jnp.float32)

def reference(activations, out_grads, residue, warm_start):
    start_basis = warm_start.astype(jnp.float32)
    tok_blocks = activations.reshape(N_DP, TOK_DEV, ROWS)
    grad_blocks = out_grads.reshape(N_DP, TOK_DEV, COLS)
    blocks = (tok_blocks, grad_blocks, residue)

    def add_left(running, pieces):
        merged = merged_of(pieces[0], pieces[1], pieces[2])
        return (running + jnp.dot(merged, start_basis, precision=highest_precision), None)
    p_raw, unused = lax.scan(add_left, jnp.zeros((ROWS, RANK), jnp.float32), blocks)
    gram_matrix = jnp.dot(p_raw.T, p_raw, precision=highest_precision)
    lower_factor = jnp.linalg.cholesky(gram_matrix)
    p_orth = whiten(lower_factor, p_raw)

    def add_right(running, pieces):
        merged = merged_of(pieces[0], pieces[1], pieces[2])
        return (running + jnp.dot(merged.T, p_orth, precision=highest_precision), None)
    factor, unused_two = lax.scan(add_right, jnp.zeros((COLS, RANK), jnp.float32), blocks)
    return jnp.dot(p_orth, factor.T, precision=highest_precision).astype(jnp.bfloat16)
```

```python
import math

import jax
import jax.numpy as jnp
from jax import lax
from jax.sharding import Mesh, PartitionSpec as P

RANK = 64
GRID = {"y": 8, "z": 8, "x": 4, "core": 2}
highest_precision = lax.Precision.HIGHEST
first_dims = (((0,), (0,)), ((), ()))
last_dims = (((1,), (1,)), ((), ()))


def dot32(left, right, dims=(((1,), (0,)), ((), ()))):
    return lax.dot_general(left, right, dims, preferred_element_type=jnp.float32)


def split(value, terms):
    parts = []
    for _ in range(terms):
        part = lax.reduce_precision(value, 8, 7)
        parts.append(part.astype(jnp.bfloat16))
        value = value - part
    return parts


def peers_of(axes):
    return math.prod(GRID[axis] for axis in axes)


def scatter_sum(value, axes):
    peers = peers_of(axes)
    chunks = value.reshape(peers, value.shape[0] // peers, value.shape[1])
    return jnp.sum(lax.all_to_all(chunks, axes, 0, 0), axis=0)


def spread(value, axes):
    copies = jnp.broadcast_to(value[None], (peers_of(axes), *value.shape))
    return lax.all_to_all(copies, axes, 0, 0)


def gather(value, axes):
    peers = peers_of(axes)
    return spread(value, axes).reshape(peers * value.shape[0], value.shape[1])


def local(activations, out_grads, residue, warm_start):
    residue = residue[0]
    projected = jnp.concatenate(split(dot32(out_grads, warm_start), 3), axis=1)
    terms = dot32(projected, activations, first_dims)
    left = terms[:RANK] + terms[RANK : 2 * RANK] + terms[2 * RANK :]
    left = left + dot32(warm_start, residue, (((0,), (1,)), ((), ())))
    left = scatter_sum(left, ("z",))
    left = jnp.sum(spread(left, ("y",)), axis=0)
    left = gather(left, ("z",))

    merged = dot32(activations, out_grads, first_dims) + residue.astype(jnp.float32)
    high, low = split(merged, 2)
    left_high, left_low = split(left, 2)
    right = dot32(left_high, high) + (dot32(left_low, high) + dot32(left_high, low))
    share = 1.0 / (GRID["y"] * GRID["z"])
    gram = lax.dot_general(left * share, left, last_dims, precision=highest_precision)
    both = jnp.concatenate([right, gram], axis=1)
    both = scatter_sum(both, ("core",))
    both = scatter_sum(both, ("z", "x"))
    both = jnp.sum(spread(both, ("y",)), axis=0)
    both = gather(both, ("z", "x"))
    both = lax.all_gather(both, "core", axis=0, tiled=True)
    right, gram = both[:, :-RANK], both[:, -RANK:]

    lower_factor = jnp.linalg.cholesky(gram)
    inverse = jax.scipy.linalg.solve_triangular(lower_factor, jnp.eye(RANK, dtype=jnp.float32), lower=True)
    whiten = lax.dot_general(inverse, inverse, first_dims, precision=highest_precision)
    scaled = lax.dot_general(left, whiten, first_dims, precision=highest_precision)
    scaled_high, scaled_low = split(scaled, 2)
    right_high, right_low = split(right, 2)
    update = dot32(
        jnp.concatenate([scaled_high, scaled_high, scaled_low], axis=1),
        jnp.concatenate([right_high, right_low, right_high], axis=0),
    )
    return update.astype(jnp.bfloat16)


def solution(mesh):
    fine = Mesh(mesh.devices.reshape(*GRID.values()), tuple(GRID))
    dp, tensor = ("y", "z"), ("x", "core")
    in_specs = (P(dp, tensor), P(dp, None), P(dp, tensor, None), P())
    return jax.shard_map(local, mesh=fine, in_specs=in_specs, out_specs=P(tensor, None), check_vma=False)
```

```python
import functools
import math

import jax
import jax.numpy as jnp
from jax import lax
from jax.experimental import pallas as pl
from jax.experimental.pallas import tpu as pltpu
from jax.sharding import Mesh, PartitionSpec as P

RANK = 64
HALF = RANK // 2
COL_BLOCK = 512
LEFT_STEPS = 4
PAIR = 2
LANES = 2 * RANK
GRAM = RANK * RANK // PAIR
GRID = {"yA": 2, "yB": 2, "yC": 2, "zA": 2, "zB": 2, "zC": 2, "x": 4, "core": 2}
DP = ("yA", "yB", "yC", "zA", "zB", "zC")
TENSOR = ("x", "core")
NEAR = ("yC", "zC")
NEAR_X = ("yC", "zC", "x")
FAR = ("yA", "yB", "zA", "zB")

highest_precision = lax.Precision.HIGHEST
plain_dims = (((1,), (0,)), ((), ()))
first_dims = (((0,), (0,)), ((), ()))
last_dims = (((1,), (1,)), ((), ()))


def dot32(left, right, dims=plain_dims):
    return lax.dot_general(left, right, dims, preferred_element_type=jnp.float32)


def dot_exact(left, right, dims=plain_dims):
    return lax.dot_general(
        left, right, dims, precision=highest_precision, preferred_element_type=jnp.float32
    )


def split(value, terms):
    parts = []
    for _ in range(terms):
        part = value.astype(jnp.bfloat16)
        parts.append(part)
        value = value - part.astype(jnp.float32)
    return parts


def params(megabytes):
    return pltpu.CompilerParams(vmem_limit_bytes=megabytes * 1024 * 1024)


def cost(flops, moved):
    return pl.CostEstimate(flops=flops, bytes_accessed=moved, transcendentals=0)


def left_kernel(act_ref, grad_ref, res_ref, warm_ref, out_ref, total, res_part):
    step = pl.program_id(0)
    warm = warm_ref[...]
    projected = jnp.concatenate(split(dot32(grad_ref[...], warm, last_dims), 3), axis=1)
    terms = dot32(projected, act_ref[...], first_dims)
    terms = terms[:RANK] + (terms[RANK : 2 * RANK] + terms[2 * RANK :])
    height = res_ref.shape[0]
    res_part[pl.ds(pl.multiple_of(step * height, 8), height), :] = dot32(res_ref[...], warm, last_dims)

    @pl.when(step == 0)
    def _():
        total[...] = terms

    @pl.when(step > 0)
    def _():
        total[...] += terms

    @pl.when(step == pl.num_programs(0) - 1)
    def _():
        out_ref[...] = total[...] + res_part[...].T


def left_product(activations, out_grads, residue, warm_start):
    tokens, rows = activations.shape
    cols = out_grads.shape[1]
    step_tokens, step_rows = tokens // LEFT_STEPS, rows // LEFT_STEPS
    return pl.pallas_call(
        left_kernel,
        grid=(LEFT_STEPS,),
        in_specs=[
            pl.BlockSpec((step_tokens, rows), lambda i: (i, 0)),
            pl.BlockSpec((step_tokens, cols), lambda i: (i, 0)),
            pl.BlockSpec((step_rows, cols), lambda i: (i, 0)),
            pl.BlockSpec((RANK, cols), lambda i: (0, 0)),
        ],
        out_specs=pl.BlockSpec((RANK, rows), lambda i: (0, 0)),
        out_shape=jax.ShapeDtypeStruct((RANK, rows), jnp.float32),
        scratch_shapes=[
            pltpu.VMEM((RANK, rows), jnp.float32),
            pltpu.VMEM((rows, RANK), jnp.float32),
        ],
        compiler_params=params(60),
        cost_estimate=cost(2 * tokens * cols * RANK, 2 * cols * (tokens + rows)),
    )(activations, out_grads, residue, warm_start.T)


def merged_kernel(act_ref, grad_ref, res_ref, high_ref, low_ref, act_t):
    @pl.when(pl.program_id(0) == 0)
    def _():
        act_t[...] = act_ref[...].T

    merged = dot32(act_t[...], grad_ref[...]) + res_ref[...].astype(jnp.float32)
    high_ref[...], low_ref[...] = split(merged, 2)


def merged_terms(activations, out_grads, residue):
    tokens, rows = activations.shape
    cols = out_grads.shape[1]
    block = pl.BlockSpec((rows, COL_BLOCK), lambda i: (0, i))
    return pl.pallas_call(
        merged_kernel,
        grid=(cols // COL_BLOCK,),
        in_specs=[
            pl.BlockSpec((tokens, rows), lambda i: (0, 0)),
            pl.BlockSpec((tokens, COL_BLOCK), lambda i: (0, i)),
            block,
        ],
        out_specs=[block, block],
        out_shape=[jax.ShapeDtypeStruct((rows, cols), jnp.bfloat16)] * 2,
        scratch_shapes=[pltpu.VMEM((rows, tokens), jnp.bfloat16)],
        compiler_params=params(36),
        cost_estimate=cost(2 * tokens * cols * rows, 2 * cols * (tokens + 3 * rows)),
    )(activations, out_grads, residue)


def right_kernel(half_ref, left_ref, high_ref, low_ref, out_ref, stacked):
    step = pl.program_id(0)
    cols = pl.num_programs(0) * COL_BLOCK

    @pl.when(step == 0)
    def _():
        start = pl.multiple_of(half_ref[0] * HALF, HALF)
        parts = split(left_ref[pl.ds(start, HALF), :], 2)
        stacked[...] = jnp.concatenate(parts, axis=0)
        left = left_ref[...]
        gram = dot_exact(left, left, last_dims)
        gram = jnp.concatenate([gram[:HALF], gram[HALF:]], axis=1)
        for i in range(HALF // PAIR):
            place = pl.ds(cols + i * LANES, LANES)
            piece = gram[i * PAIR : (i + 1) * PAIR, :]
            out_ref[:, :, place] = jnp.broadcast_to(piece[None], (HALF // PAIR, PAIR, LANES))

    both = dot32(stacked[...], high_ref[...])
    small = dot32(stacked[:HALF], low_ref[...])
    place = pl.ds(pl.multiple_of(step * COL_BLOCK, COL_BLOCK), COL_BLOCK)
    product = both[:HALF] + (both[HALF:] + small)
    out_ref[:, :, place] = product.reshape(HALF // PAIR, PAIR, COL_BLOCK)


def right_product(half, left, high, low):
    rows, cols = high.shape
    shape = (HALF // PAIR, PAIR, cols + GRAM)
    block = pl.BlockSpec((rows, COL_BLOCK), lambda i: (0, i))
    return pl.pallas_call(
        right_kernel,
        grid=(cols // COL_BLOCK,),
        in_specs=[
            pl.BlockSpec(memory_space=pltpu.SMEM),
            pl.BlockSpec((RANK, rows), lambda i: (0, 0)),
            block,
            block,
        ],
        out_specs=pl.BlockSpec(shape, lambda i: (0, 0, 0)),
        out_shape=jax.ShapeDtypeStruct(shape, jnp.float32),
        scratch_shapes=[pltpu.VMEM((2 * HALF, rows), jnp.bfloat16)],
        compiler_params=params(16),
        cost_estimate=cost(6 * rows * cols * HALF, 4 * cols * rows),
    )(half, left, high, low)


def whiten_kernel(copies, gram_ref, left_ref, out_ref):
    first = gram_ref.shape[1] - GRAM
    gram = jnp.concatenate(
        [gram_ref[:, first + i * LANES : first + (i + 1) * LANES] for i in range(HALF // PAIR)], axis=0
    )
    gram = jnp.concatenate([gram[:, :RANK], gram[:, RANK:]], axis=0) * (1.0 / copies)
    row = lax.broadcasted_iota(jnp.int32, (RANK, RANK), 0)
    col = lax.broadcasted_iota(jnp.int32, (RANK, RANK), 1)
    work = jnp.concatenate([gram, (row == col).astype(jnp.float32)], axis=1)
    tall = lax.broadcasted_iota(jnp.int32, (RANK, 2 * RANK), 0)
    for k in range(RANK - 1):
        pivot = work[k : k + 1, :]
        scale = work[:, k : k + 1] / pivot[:, k : k + 1]
        work = jnp.where(tall > k, work - scale * pivot, work)
    inverse = work[:, RANK:]
    diagonal = jnp.sum(jnp.where(row == col, work[:, :RANK], 0.0), axis=1, keepdims=True)
    basis = dot_exact(inverse, left_ref[...])
    scaled = dot_exact(basis, inverse / diagonal, first_dims)
    high, low = split(scaled, 2)
    out_ref[...] = jnp.concatenate([high, high, low], axis=1)


def whiten(right, left):
    rows = left.shape[1]
    return pl.pallas_call(
        functools.partial(whiten_kernel, peers_of(NEAR)),
        out_shape=jax.ShapeDtypeStruct((rows, 3 * RANK), jnp.bfloat16),
        compiler_params=params(16),
        cost_estimate=cost(400_000_000, 4_000_000),
    )(right, left)


def update_kernel(scaled_ref, right_ref, out_ref):
    right = right_ref[...].reshape(RANK, out_ref.shape[1])
    high, low = split(right, 2)
    terms = jnp.concatenate([high, low, high], axis=0)
    out_ref[...] = dot32(scaled_ref[...], terms).astype(jnp.bfloat16)


def update_product(scaled, right):
    rows, cols = scaled.shape[0], right.shape[-1]
    return pl.pallas_call(
        update_kernel,
        grid=(cols // COL_BLOCK,),
        in_specs=[
            pl.BlockSpec(scaled.shape, lambda i: (0, 0)),
            pl.BlockSpec((2, HALF // PAIR, PAIR, COL_BLOCK), lambda i: (0, 0, 0, i)),
        ],
        out_specs=pl.BlockSpec((rows, COL_BLOCK), lambda i: (0, i)),
        out_shape=jax.ShapeDtypeStruct((rows, cols), jnp.bfloat16),
        compiler_params=params(16),
        cost_estimate=cost(6 * rows * cols * RANK, 2 * cols * rows),
    )(scaled, right)


def peers_of(axes):
    return math.prod(GRID[axis] for axis in axes)


def scatter_sum(chunks, axes):
    return jnp.sum(lax.all_to_all(chunks, axes, 0, 0), axis=0)


def spread(value, axes):
    copies = jnp.broadcast_to(value[None], (peers_of(axes), *value.shape))
    return lax.all_to_all(copies, axes, 0, 0)


def after(first, *values):
    return lax.optimization_barrier((first, *values))


def local(activations, out_grads, residue, warm_start):
    residue = residue[0]
    left = left_product(activations, out_grads, residue, warm_start)
    left = scatter_sum(left.reshape(peers_of(NEAR), -1, left.shape[1]), NEAR)
    left, activations = after(left, activations)
    high, low = merged_terms(activations, out_grads, residue)
    left = jnp.sum(spread(left, FAR), axis=0)
    left, high, low = after(left, high, low)
    left = spread(left, NEAR).reshape(RANK, -1)

    core = lax.axis_index("core").astype(jnp.int32).reshape(1)
    sent = right_product(1 - core, left, high, low)
    kept = right_product(core, left, high, low)
    both = kept + lax.ppermute(sent, "core", [(0, 1), (1, 0)])
    right = scatter_sum(both, NEAR_X)
    scaled = whiten(right, left)
    right = jnp.sum(spread(right[:, : high.shape[1]], FAR), axis=0)
    right, scaled = after(right, scaled)
    right = lax.all_gather(spread(right, NEAR_X), "core", axis=0)
    return update_product(scaled, right)


def solution(mesh):
    fine = Mesh(mesh.devices.reshape(*GRID.values()), tuple(GRID))
    in_specs = (P(DP, TENSOR), P(DP, None), P(DP, TENSOR, None), P())
    return jax.shard_map(local, mesh=fine, in_specs=in_specs, out_specs=P(TENSOR, None), check_vma=False)
```

```python
import math

import jax
import jax.numpy as jnp
from jax import lax
from jax.experimental import pallas as pl
from jax.experimental.pallas import tpu as pltpu
from jax.sharding import Mesh, PartitionSpec as P

RANK = 64
HALF = RANK // 2
LANES = 2 * RANK
PARTS = 2
GRID = {"yA": 2, "yB": 2, "yC": 2, "zA": 2, "zB": 2, "zC": 2, "x": 4, "core": 2}
DP = ("yA", "yB", "yC", "zA", "zB", "zC")
TENSOR = ("x", "core")
Y, Z = DP[:3], DP[3:]
NEAR = ("yC", "zC")
NEAR_X = ("yC", "zC", "x")
FAR = ("yA", "yB", "zA", "zB")

highest_precision = lax.Precision.HIGHEST
plain_dims = (((1,), (0,)), ((), ()))
first_dims = (((0,), (0,)), ((), ()))
last_dims = (((1,), (1,)), ((), ()))


def dot32(left, right, dims=plain_dims):
    return lax.dot_general(left, right, dims, preferred_element_type=jnp.float32)


def dot_exact(left, right, dims=plain_dims):
    return lax.dot_general(
        left, right, dims, precision=highest_precision, preferred_element_type=jnp.float32
    )


def split(value, terms):
    parts = []
    for _ in range(terms):
        part = lax.reduce_precision(value, 8, 7)
        parts.append(part.astype(jnp.bfloat16))
        value = value - part
    return parts


def kernel_split(value, terms):
    parts = []
    for _ in range(terms):
        part = value.astype(jnp.bfloat16)
        parts.append(part)
        value = value - part.astype(jnp.float32)
    return parts


def peers_of(axes):
    return math.prod(GRID[axis] for axis in axes)


def params(megabytes):
    return pltpu.CompilerParams(vmem_limit_bytes=megabytes * 1024 * 1024)


def cost(flops, moved):
    return pl.CostEstimate(flops=flops, bytes_accessed=moved, transcendentals=0)


WHOLE = pl.BlockSpec(memory_space=pltpu.VMEM)


def left_product(activations, out_grads, residue, warm_start):
    projected = jnp.concatenate(split(dot32(out_grads, warm_start), 3), axis=1)
    terms = dot32(projected, activations, first_dims)
    left = terms[:RANK] + terms[RANK : 2 * RANK] + terms[2 * RANK :]
    return left + dot32(warm_start, residue, (((0,), (1,)), ((), ())))


def merged_kernel(act_ref, grad_ref, res_ref, out_ref, act_t):
    @pl.when(pl.program_id(0) == 0)
    def _():
        act_t[...] = act_ref[...].T

    merged = dot32(act_t[...], grad_ref[...]) + res_ref[...].astype(jnp.float32)
    out_ref[0], out_ref[1] = kernel_split(merged, 2)


def merged_terms(activations, out_grads, residue, part):
    tokens, rows = activations.shape
    cols = out_grads.shape[1] // PARTS
    steps = 2
    block, first = cols // steps, part * steps
    return pl.pallas_call(
        merged_kernel,
        grid=(steps,),
        in_specs=[
            pl.BlockSpec((tokens, rows), lambda i: (0, 0)),
            pl.BlockSpec((tokens, block), lambda i: (0, first + i)),
            pl.BlockSpec((rows, block), lambda i: (0, first + i)),
        ],
        out_specs=pl.BlockSpec((2, rows, block), lambda i: (0, 0, i)),
        out_shape=jax.ShapeDtypeStruct((2, rows, cols), jnp.bfloat16),
        scratch_shapes=[pltpu.VMEM((rows, tokens), jnp.bfloat16)],
        compiler_params=params(60),
        cost_estimate=cost(2 * tokens * cols * rows, 2 * cols * (tokens + 3 * rows)),
    )(activations, out_grads, residue)


def right_kernel(left_ref, *refs):
    *terms_refs, kept_ref, sent_ref = refs
    cols = sum(terms_ref.shape[2] for terms_ref in terms_refs)
    peers, pair, _ = kept_ref.shape
    left = left_ref[...]
    swapped = jnp.concatenate([left[HALF:], left[:HALF]], axis=0)
    high, low = kernel_split(jnp.where(lax.axis_index("core") == 0, left, swapped), 2)
    stacked = jnp.concatenate([high, low], axis=0)
    block = terms_refs[0].shape[2] // 2
    for i in range(cols // block):
        terms_ref, place = terms_refs[i // 2], slice(i % 2 * block, (i % 2 + 1) * block)
        both = dot32(stacked, terms_ref[0, :, place])
        product = both[:RANK] + (both[RANK:] + dot32(high, terms_ref[1, :, place]))
        place = slice(i * block, (i + 1) * block)
        kept_ref[:, :, place] = product[:HALF].reshape(peers, pair, block)
        sent_ref[:, :, place] = product[HALF:].reshape(peers, pair, block)

    gram = dot_exact(left, left, last_dims)
    gram = jnp.concatenate([gram[:HALF], gram[HALF:]], axis=1)
    shares = peers_of(NEAR)
    height = HALF // shares
    share = gram[:height]
    mine = lax.axis_index(NEAR)
    for other in range(1, shares):
        share = jnp.where(mine == other, gram[other * height : (other + 1) * height], share)
    for i in range(height // pair):
        place = slice(cols + i * LANES, cols + (i + 1) * LANES)
        piece = jnp.broadcast_to(share[i * pair : (i + 1) * pair][None], (peers, pair, LANES))
        kept_ref[:, :, place] = piece
        sent_ref[:, :, place] = piece


def right_product(left, terms):
    rows, cols = left.shape[1], sum(part.shape[2] for part in terms)
    peers = peers_of(NEAR_X)
    shape = (peers, HALF // peers, cols + LANES * GRID["x"])
    return pl.pallas_call(
        right_kernel,
        in_specs=[WHOLE] * (1 + len(terms)),
        out_specs=[WHOLE] * 2,
        out_shape=[jax.ShapeDtypeStruct(shape, jnp.float32)] * 2,
        compiler_params=params(16),
        cost_estimate=cost(6 * rows * cols * RANK, 4 * cols * rows),
    )(left, *terms)


def whiten_kernel(gram_ref, left_ref, out_ref):
    shares, sources, pair = peers_of(NEAR), GRID["x"], gram_ref.shape[1]
    pieces = []
    for share in range(shares):
        for i in range(HALF // shares // pair):
            place = slice(i * LANES, (i + 1) * LANES)
            first = share * sources
            piece = gram_ref[first, :, place]
            for source in range(1, sources):
                piece = piece + gram_ref[first + source, :, place]
            pieces.append(piece)
    gram = jnp.concatenate(pieces, axis=0)
    gram = jnp.concatenate([gram[:, :RANK], gram[:, RANK:]], axis=0)
    row = lax.broadcasted_iota(jnp.int32, (RANK, RANK), 0)
    col = lax.broadcasted_iota(jnp.int32, (RANK, RANK), 1)
    work = jnp.concatenate([gram, (row == col).astype(jnp.float32)], axis=1)
    tall = lax.broadcasted_iota(jnp.int32, (RANK, 2 * RANK), 0)
    for k in range(RANK - 1):
        pivot = work[k : k + 1, :]
        scale = work[:, k : k + 1] / pivot[:, k : k + 1]
        work = jnp.where(tall > k, work - scale * pivot, work)
    inverse = work[:, RANK:]
    diagonal = jnp.sum(jnp.where(row == col, work[:, :RANK], 0.0), axis=1, keepdims=True)
    basis = dot_exact(inverse, left_ref[...])
    scaled = dot_exact(basis, inverse / diagonal, first_dims)
    high, low = kernel_split(scaled, 2)
    out_ref[...] = jnp.concatenate([high, high, low], axis=1)


def whiten(chunks, left):
    rows = left.shape[1]
    width = LANES * GRID["x"]
    last = chunks.shape[2] // width - 1
    return pl.pallas_call(
        whiten_kernel,
        grid=(1,),
        in_specs=[
            pl.BlockSpec((*chunks.shape[:2], width), lambda i: (0, 0, last)),
            pl.BlockSpec(left.shape, lambda i: (0, 0)),
        ],
        out_specs=pl.BlockSpec((rows, 3 * RANK), lambda i: (0, 0)),
        out_shape=jax.ShapeDtypeStruct((rows, 3 * RANK), jnp.bfloat16),
        compiler_params=params(16),
        cost_estimate=cost(400_000_000, 4_000_000),
    )(chunks, left)


def update_kernel(scaled_ref, right_ref, out_ref, held, sems):
    block = 512
    copies = []
    for i in range(held.shape[1] // block):
        place = slice(i * block, (i + 1) * block)
        high, low = kernel_split(right_ref[:, :, :, place].reshape(RANK, block), 2)
        terms = jnp.concatenate([high, low, high], axis=0)
        held[:, place] = dot32(scaled_ref[...], terms).astype(jnp.bfloat16)
        place = pl.ds(i * block, block)
        copies.append(pltpu.make_async_copy(held.at[:, place], out_ref.at[:, place], sems.at[i]))
        copies[-1].start()
    for copy in copies:
        copy.wait()


def update_product(scaled, right):
    rows, cols = scaled.shape[0], right.shape[-1]
    return pl.pallas_call(
        update_kernel,
        in_specs=[WHOLE] * 2,
        out_specs=pl.BlockSpec(memory_space=pl.ANY),
        out_shape=jax.ShapeDtypeStruct((rows, cols), jnp.bfloat16),
        scratch_shapes=[
            pltpu.VMEM((rows, cols), jnp.bfloat16),
            pltpu.SemaphoreType.DMA((cols // 512,)),
        ],
        compiler_params=params(16),
        cost_estimate=cost(6 * rows * cols * RANK, 2 * cols * rows),
    )(scaled, right)


def copies_kernel(chunks_ref, out_ref):
    total = chunks_ref[0]
    for peer in range(1, chunks_ref.shape[0]):
        total = total + chunks_ref[peer]
    for peer in range(out_ref.shape[0]):
        out_ref[peer] = total


def sum_copies(chunks, axes, cols):
    sources, rows, _ = chunks.shape
    shape = (peers_of(axes), rows, cols)
    return pl.pallas_call(
        copies_kernel,
        grid=(1,),
        in_specs=[pl.BlockSpec((sources, rows, cols), lambda i: (0, 0, 0))],
        out_specs=pl.BlockSpec(shape, lambda i: (0, 0, 0)),
        out_shape=pltpu.VMEM(shape, jnp.float32),
        compiler_params=params(8),
        cost_estimate=cost(sources * rows * cols, 4 * sources * rows * cols),
    )(chunks)


def exchange(chunks, axes):
    return lax.all_to_all(chunks, axes, 0, 0)


def after(first, *values):
    return lax.optimization_barrier((first, *values))


def local(activations, out_grads, residue, warm_start):
    residue = residue[0]
    rows, cols = residue.shape
    core = lax.axis_index("core")
    left = left_product(activations, out_grads, residue, warm_start)
    left, activations, is_first = after(left, activations, core == 0)
    terms_a = merged_terms(activations, out_grads, residue, 0)
    left = exchange(left.reshape(peers_of(Z), -1, rows), Z)
    left, terms_a, activations = after(sum_copies(left, Y, rows), terms_a, activations)
    terms_b = merged_terms(activations, out_grads, residue, 1)
    left, terms_b = after(sum_copies(exchange(left, Y), Z, rows), terms_b)
    left = exchange(left, Z).reshape(RANK, rows)

    kept, sent = right_product(left, [terms_a, terms_b])
    sent = lax.all_gather(sent, "core", axis=0)
    chunks = exchange(kept + jnp.where(is_first, sent[1], sent[0]), NEAR_X)
    scaled = whiten(chunks, left)
    right = exchange(sum_copies(chunks, FAR, cols), FAR)
    right, scaled = after(sum_copies(right, NEAR_X, cols), scaled)
    right = lax.all_gather(exchange(right, NEAR_X), "core", axis=0)
    return update_product(scaled, right)


def solution(mesh):
    fine = Mesh(mesh.devices.reshape(*GRID.values()), tuple(GRID))
    in_specs = (P(DP, TENSOR), P(DP, None), P(DP, TENSOR, None), P())
    return jax.shard_map(local, mesh=fine, in_specs=in_specs, out_specs=P(TENSOR, None), check_vma=False)
```

```python
import math

import jax
import jax.numpy as jnp
from jax import lax
from jax.experimental import pallas as pl
from jax.experimental.pallas import tpu as pltpu
from jax.sharding import Mesh, PartitionSpec as P

RANK = 64
HALF = RANK // 2
LANES = 2 * RANK
GRAD_BLOCKS = 2
GRID = {"yA": 2, "yB": 2, "yC": 2, "zA": 2, "zB": 2, "zC": 2, "x": 4, "core": 2}
DP = ("yA", "yB", "yC", "zA", "zB", "zC")
TENSOR = ("x", "core")
Y, Z = DP[:3], DP[3:]
NEAR = ("yC", "zC")
NEAR_X = ("yC", "zC", "x")
FAR = ("yA", "yB", "zA", "zB")

highest_precision = lax.Precision.HIGHEST
plain_dims = (((1,), (0,)), ((), ()))
first_dims = (((0,), (0,)), ((), ()))
last_dims = (((1,), (1,)), ((), ()))


def dot32(left, right, dims=plain_dims):
    return lax.dot_general(left, right, dims, preferred_element_type=jnp.float32)


def dot_exact(left, right, dims=plain_dims):
    return lax.dot_general(
        left, right, dims, precision=highest_precision, preferred_element_type=jnp.float32
    )


def split(value, terms):
    parts = []
    for _ in range(terms):
        part = lax.reduce_precision(value, 8, 7)
        parts.append(part.astype(jnp.bfloat16))
        value = value - part
    return parts


def kernel_split(value, terms):
    parts = []
    for _ in range(terms):
        part = value.astype(jnp.bfloat16)
        parts.append(part)
        value = value - part.astype(jnp.float32)
    return parts


def peers_of(axes):
    return math.prod(GRID[axis] for axis in axes)


def params(megabytes):
    return pltpu.CompilerParams(vmem_limit_bytes=megabytes * 1024 * 1024)


def cost(flops, moved):
    return pl.CostEstimate(flops=flops, bytes_accessed=moved, transcendentals=0)


WHOLE = pl.BlockSpec(memory_space=pltpu.VMEM)


def left_kernel(act_hbm, grad_hbm, res_hbm, warm_hbm, out_ref, act_ref, grad_ref, res_ref, warm_ref, sems):
    tokens = grad_ref.shape[0]
    block = tokens // GRAD_BLOCKS
    places = [pl.ds(i * block, block) for i in range(GRAD_BLOCKS)]
    moves = [(warm_hbm, warm_ref), (res_hbm, res_ref)]
    moves += [(grad_hbm.at[place], grad_ref.at[place]) for place in places]
    moves += [(act_hbm, act_ref)]
    copies = [pltpu.make_async_copy(*move, sems.at[i]) for i, move in enumerate(moves)]
    for copy in copies:
        copy.start()
    copies[0].wait()
    warm = warm_ref[...]
    copies[1].wait()
    left = dot32(warm, res_ref[...], last_dims)
    projected = []
    for i, place in enumerate(places):
        copies[2 + i].wait()
        terms = kernel_split(dot32(warm, grad_ref[place, :], last_dims), 3)
        projected.append(jnp.concatenate(terms, axis=0))
    copies[-1].wait()
    terms = dot32(jnp.concatenate(projected, axis=1), act_ref[...])
    out_ref[...] = terms[:RANK] + (terms[RANK : 2 * RANK] + terms[2 * RANK :]) + left


def left_product(activations, out_grads, residue, warm_start):
    tokens, rows = activations.shape
    cols = out_grads.shape[1]
    arrays = [activations, out_grads, residue, warm_start.T]
    held = [pltpu.VMEM(array.shape, array.dtype) for array in arrays[:3]]
    return pl.pallas_call(
        left_kernel,
        in_specs=[pl.BlockSpec(memory_space=pltpu.HBM)] * 4,
        out_specs=[WHOLE] * 4,
        out_shape=[pltpu.VMEM((RANK, rows), jnp.float32), *held],
        scratch_shapes=[
            pltpu.VMEM((RANK, cols), warm_start.dtype),
            pltpu.SemaphoreType.DMA((3 + GRAD_BLOCKS,)),
        ],
        compiler_params=params(16),
        cost_estimate=cost(2 * tokens * cols * RANK, 2 * cols * (tokens + rows)),
    )(*[pltpu.with_memory_space_constraint(array, pltpu.HBM) for array in arrays])


def right_kernel(left_ref, act_ref, grad_ref, res_ref, kept_ref, sent_ref):
    cols = grad_ref.shape[1]
    peers, pair, _ = kept_ref.shape
    left = left_ref[...]
    swapped = jnp.concatenate([left[HALF:], left[:HALF]], axis=0)
    ordered = kernel_split(jnp.where(lax.axis_index("core") == 0, left, swapped), 2)
    ordered = jnp.concatenate(ordered, axis=0)
    inner = dot32(ordered, act_ref[...], last_dims)
    inner = jnp.concatenate(kernel_split(inner[:RANK] + inner[RANK:], 2), axis=0)
    block = 512
    for start in range(0, cols, block):
        place = slice(start, start + block)
        terms = dot32(inner, grad_ref[:, place]) + dot32(ordered, res_ref[:, place])
        product = terms[:RANK] + terms[RANK:]
        kept_ref[:, :, place] = product[:HALF].reshape(peers, pair, block)
        sent_ref[:, :, place] = product[HALF:].reshape(peers, pair, block)

    gram = dot_exact(left, left, last_dims)
    gram = jnp.concatenate([gram[:HALF], gram[HALF:]], axis=1)
    shares = peers_of(NEAR)
    height = HALF // shares
    share = gram[:height]
    mine = lax.axis_index(NEAR)
    for other in range(1, shares):
        share = jnp.where(mine == other, gram[other * height : (other + 1) * height], share)
    for i in range(height // pair):
        place = slice(cols + i * LANES, cols + (i + 1) * LANES)
        piece = jnp.broadcast_to(share[i * pair : (i + 1) * pair][None], (peers, pair, LANES))
        kept_ref[:, :, place] = piece
        sent_ref[:, :, place] = piece


def right_product(left, activations, out_grads, residue):
    (rows, cols), tokens = residue.shape, out_grads.shape[0]
    peers = peers_of(NEAR_X)
    shape = (peers, HALF // peers, cols + LANES * GRID["x"])
    return pl.pallas_call(
        right_kernel,
        in_specs=[WHOLE] * 4,
        out_specs=[WHOLE] * 2,
        out_shape=[jax.ShapeDtypeStruct(shape, jnp.float32)] * 2,
        compiler_params=params(16),
        cost_estimate=cost(4 * (tokens + rows) * cols * RANK, 2 * cols * (tokens + rows)),
    )(left, activations, out_grads, residue)


def whiten_kernel(gram_ref, left_ref, out_ref):
    shares, sources, pair = peers_of(NEAR), GRID["x"], gram_ref.shape[1]
    pieces = []
    for share in range(shares):
        for i in range(HALF // shares // pair):
            place = slice(i * LANES, (i + 1) * LANES)
            first = share * sources
            piece = gram_ref[first, :, place]
            for source in range(1, sources):
                piece = piece + gram_ref[first + source, :, place]
            pieces.append(piece)
    gram = jnp.concatenate(pieces, axis=0)
    gram = jnp.concatenate([gram[:, :RANK], gram[:, RANK:]], axis=0)
    row = lax.broadcasted_iota(jnp.int32, (RANK, RANK), 0)
    col = lax.broadcasted_iota(jnp.int32, (RANK, RANK), 1)
    work = jnp.concatenate([gram, (row == col).astype(jnp.float32)], axis=1)
    tall = lax.broadcasted_iota(jnp.int32, (RANK, 2 * RANK), 0)
    for k in range(RANK - 1):
        pivot = work[k : k + 1, :]
        scale = work[:, k : k + 1] / pivot[:, k : k + 1]
        work = jnp.where(tall > k, work - scale * pivot, work)
    inverse = work[:, RANK:]
    diagonal = jnp.sum(jnp.where(row == col, work[:, :RANK], 0.0), axis=1, keepdims=True)
    basis = dot_exact(inverse, left_ref[...])
    scaled = dot_exact(basis, inverse / diagonal, first_dims)
    high, low = kernel_split(scaled, 2)
    out_ref[...] = jnp.concatenate([high, high, low], axis=1)


def whiten(chunks, left):
    rows = left.shape[1]
    width = LANES * GRID["x"]
    last = chunks.shape[2] // width - 1
    return pl.pallas_call(
        whiten_kernel,
        grid=(1,),
        in_specs=[
            pl.BlockSpec((*chunks.shape[:2], width), lambda i: (0, 0, last)),
            pl.BlockSpec(left.shape, lambda i: (0, 0)),
        ],
        out_specs=pl.BlockSpec((rows, 3 * RANK), lambda i: (0, 0)),
        out_shape=jax.ShapeDtypeStruct((rows, 3 * RANK), jnp.bfloat16),
        compiler_params=params(16),
        cost_estimate=cost(400_000_000, 4_000_000),
    )(chunks, left)


def update_kernel(scaled_ref, right_ref, out_ref, held, sems):
    block = 512
    copies = []
    for i in range(held.shape[1] // block):
        place = slice(i * block, (i + 1) * block)
        high, low = kernel_split(right_ref[:, :, :, place].reshape(RANK, block), 2)
        terms = jnp.concatenate([high, low, high], axis=0)
        held[:, place] = dot32(scaled_ref[...], terms).astype(jnp.bfloat16)
        place = pl.ds(i * block, block)
        copies.append(pltpu.make_async_copy(held.at[:, place], out_ref.at[:, place], sems.at[i]))
        copies[-1].start()
    for copy in copies:
        copy.wait()


def update_product(scaled, right):
    rows, cols = scaled.shape[0], right.shape[-1]
    return pl.pallas_call(
        update_kernel,
        in_specs=[WHOLE] * 2,
        out_specs=pl.BlockSpec(memory_space=pl.ANY),
        out_shape=jax.ShapeDtypeStruct((rows, cols), jnp.bfloat16),
        scratch_shapes=[
            pltpu.VMEM((rows, cols), jnp.bfloat16),
            pltpu.SemaphoreType.DMA((cols // 512,)),
        ],
        compiler_params=params(16),
        cost_estimate=cost(6 * rows * cols * RANK, 2 * cols * rows),
    )(scaled, right)


def copies_kernel(chunks_ref, out_ref):
    total = chunks_ref[0]
    for peer in range(1, chunks_ref.shape[0]):
        total = total + chunks_ref[peer]
    for peer in range(out_ref.shape[0]):
        out_ref[peer] = total


def sum_copies(chunks, axes, cols):
    sources, rows, _ = chunks.shape
    shape = (peers_of(axes), rows, cols)
    return pl.pallas_call(
        copies_kernel,
        grid=(1,),
        in_specs=[pl.BlockSpec((sources, rows, cols), lambda i: (0, 0, 0))],
        out_specs=pl.BlockSpec(shape, lambda i: (0, 0, 0)),
        out_shape=pltpu.VMEM(shape, jnp.float32),
        compiler_params=params(8),
        cost_estimate=cost(sources * rows * cols, 4 * sources * rows * cols),
    )(chunks)


def exchange(chunks, axes):
    return lax.all_to_all(chunks, axes, 0, 0)


def after(first, *values):
    return lax.optimization_barrier((first, *values))


def local(activations, out_grads, residue, warm_start):
    residue = residue[0]
    rows, cols = residue.shape
    is_first = lax.axis_index("core") == 0
    left, *held = left_product(activations, out_grads, residue, warm_start)
    left, is_first = after(left, is_first)
    left = sum_copies(exchange(left.reshape(peers_of(Z), -1, rows), Z), Y, rows)
    left = sum_copies(exchange(left, Y), Z, rows)
    left = exchange(left, Z).reshape(RANK, rows)

    kept, sent = right_product(left, *held)
    sent = lax.all_gather(sent, "core", axis=0)
    chunks = exchange(kept + jnp.where(is_first, sent[1], sent[0]), NEAR_X)
    scaled = whiten(chunks, left)
    right = exchange(sum_copies(chunks, FAR, cols), FAR)
    right, scaled = after(sum_copies(right, NEAR_X, cols), scaled)
    right = lax.all_gather(exchange(right, NEAR_X), "core", axis=0)
    return update_product(scaled, right)


def solution(mesh):
    fine = Mesh(mesh.devices.reshape(*GRID.values()), tuple(GRID))
    in_specs = (P(DP, TENSOR), P(DP, None), P(DP, TENSOR, None), P())
    return jax.shard_map(local, mesh=fine, in_specs=in_specs, out_specs=P(TENSOR, None), check_vma=False)
```

```python
import math

import jax
import jax.numpy as jnp
from jax import lax
from jax.experimental import pallas as pl
from jax.experimental.pallas import tpu as pltpu
from jax.sharding import Mesh, PartitionSpec as P

RANK = 64
HALF = RANK // 2
LANES = 2 * RANK
GRAD_BLOCKS = 2
GRID = {"yA": 2, "yB": 2, "yC": 2, "zA": 2, "zB": 2, "zC": 2, "xA": 2, "xB": 2, "core": 2}
DP = ("yA", "yB", "yC", "zA", "zB", "zC")
TENSOR = ("xA", "xB", "core")
LEFT_NEAR, LEFT_FAR = ("zC", "zB", "zA"), ("yC", "yB", "yA")
NEAR = ("zC", "yC")
X = ("xB", "xA")
NEAR_X = (*X, "zC", "yC")
FAR = ("zB", "zA", "yA", "yB")

highest_precision = lax.Precision.HIGHEST
plain_dims = (((1,), (0,)), ((), ()))
first_dims = (((0,), (0,)), ((), ()))
last_dims = (((1,), (1,)), ((), ()))


def dot32(left, right, dims=plain_dims):
    return lax.dot_general(left, right, dims, preferred_element_type=jnp.float32)


def dot_exact(left, right, dims=plain_dims):
    return lax.dot_general(
        left, right, dims, precision=highest_precision, preferred_element_type=jnp.float32
    )


def split(value, terms):
    parts = []
    for _ in range(terms):
        part = lax.reduce_precision(value, 8, 7)
        parts.append(part.astype(jnp.bfloat16))
        value = value - part
    return parts


def kernel_split(value, terms):
    parts = []
    for _ in range(terms):
        part = value.astype(jnp.bfloat16)
        parts.append(part)
        value = value - part.astype(jnp.float32)
    return parts


def peers_of(axes):
    return math.prod(GRID[axis] for axis in axes)


def params(megabytes):
    return pltpu.CompilerParams(vmem_limit_bytes=megabytes * 1024 * 1024)


def cost(flops, moved):
    return pl.CostEstimate(flops=flops, bytes_accessed=moved, transcendentals=0)


WHOLE = pl.BlockSpec(memory_space=pltpu.VMEM)


def left_kernel(act_hbm, grad_hbm, res_hbm, warm_hbm, out_ref, act_ref, grad_ref, res_ref, warm_ref, sems):
    tokens = grad_ref.shape[0]
    block = tokens // GRAD_BLOCKS
    places = [pl.ds(i * block, block) for i in range(GRAD_BLOCKS)]
    moves = [(warm_hbm, warm_ref), (res_hbm, res_ref)]
    moves += [(grad_hbm.at[place], grad_ref.at[place]) for place in places]
    moves += [(act_hbm, act_ref)]
    copies = [pltpu.make_async_copy(*move, sems.at[i]) for i, move in enumerate(moves)]
    for copy in copies:
        copy.start()
    copies[0].wait()
    warm = warm_ref[...]
    copies[1].wait()
    left = dot32(warm, res_ref[...], last_dims)
    projected = []
    for i, place in enumerate(places):
        copies[2 + i].wait()
        terms = kernel_split(dot32(warm, grad_ref[place, :], last_dims), 3)
        projected.append(jnp.concatenate(terms, axis=0))
    copies[-1].wait()
    terms = dot32(jnp.concatenate(projected, axis=1), act_ref[...])
    out_ref[...] = terms[:RANK] + (terms[RANK : 2 * RANK] + terms[2 * RANK :]) + left


def left_product(activations, out_grads, residue, warm_start):
    tokens, rows = activations.shape
    cols = out_grads.shape[1]
    arrays = [activations, out_grads, residue, warm_start.T]
    held = [pltpu.VMEM(array.shape, array.dtype) for array in arrays[:3]]
    return pl.pallas_call(
        left_kernel,
        in_specs=[pl.BlockSpec(memory_space=pltpu.HBM)] * 4,
        out_specs=[WHOLE] * 4,
        out_shape=[pltpu.VMEM((RANK, rows), jnp.float32), *held],
        scratch_shapes=[
            pltpu.VMEM((RANK, cols), warm_start.dtype),
            pltpu.SemaphoreType.DMA((3 + GRAD_BLOCKS,)),
        ],
        compiler_params=params(16),
        cost_estimate=cost(2 * tokens * cols * RANK, 2 * cols * (tokens + rows)),
    )(*[pltpu.with_memory_space_constraint(array, pltpu.HBM) for array in arrays])


def right_kernel(left_ref, act_ref, grad_ref, res_ref, kept_ref, sent_ref):
    cols = grad_ref.shape[1]
    peers, pair, _ = kept_ref.shape
    left = left_ref[...]
    swapped = jnp.concatenate([left[HALF:], left[:HALF]], axis=0)
    ordered = kernel_split(jnp.where(lax.axis_index("core") == 0, left, swapped), 2)
    ordered = jnp.concatenate(ordered, axis=0)
    inner = dot32(ordered, act_ref[...], last_dims)
    inner = jnp.concatenate(kernel_split(inner[:RANK] + inner[RANK:], 2), axis=0)
    block = 512
    for start in range(0, cols, block):
        place = slice(start, start + block)
        terms = dot32(inner, grad_ref[:, place]) + dot32(ordered, res_ref[:, place])
        product = terms[:RANK] + terms[RANK:]
        kept_ref[:, :, place] = product[:HALF].reshape(peers, pair, block)
        sent_ref[:, :, place] = product[HALF:].reshape(peers, pair, block)

    gram = dot_exact(left, left, last_dims)
    gram = jnp.concatenate([gram[:HALF], gram[HALF:]], axis=1)
    shares = peers_of(NEAR)
    height = HALF // shares
    share = gram[:height]
    mine = lax.axis_index(NEAR)
    for other in range(1, shares):
        share = jnp.where(mine == other, gram[other * height : (other + 1) * height], share)
    for i in range(height // pair):
        place = slice(cols + i * LANES, cols + (i + 1) * LANES)
        piece = jnp.broadcast_to(share[i * pair : (i + 1) * pair][None], (peers, pair, LANES))
        kept_ref[:, :, place] = piece
        sent_ref[:, :, place] = piece


def right_product(left, activations, out_grads, residue):
    (rows, cols), tokens = residue.shape, out_grads.shape[0]
    peers = peers_of(NEAR_X)
    shape = (peers, HALF // peers, cols + LANES * peers_of(X))
    return pl.pallas_call(
        right_kernel,
        in_specs=[WHOLE] * 4,
        out_specs=[WHOLE] * 2,
        out_shape=[jax.ShapeDtypeStruct(shape, jnp.float32)] * 2,
        compiler_params=params(16),
        cost_estimate=cost(4 * (tokens + rows) * cols * RANK, 2 * cols * (tokens + rows)),
    )(left, activations, out_grads, residue)


def whiten_kernel(gram_ref, left_ref, out_ref):
    shares, sources, pair = peers_of(NEAR), peers_of(X), gram_ref.shape[1]
    pieces = []
    for share in range(shares):
        for i in range(HALF // shares // pair):
            place = slice(i * LANES, (i + 1) * LANES)
            piece = gram_ref[share, :, place]
            for source in range(1, sources):
                piece = piece + gram_ref[source * shares + share, :, place]
            pieces.append(piece)
    gram = jnp.concatenate(pieces, axis=0)
    gram = jnp.concatenate([gram[:, :RANK], gram[:, RANK:]], axis=0)
    row = lax.broadcasted_iota(jnp.int32, (RANK, RANK), 0)
    col = lax.broadcasted_iota(jnp.int32, (RANK, RANK), 1)
    work = jnp.concatenate([gram, (row == col).astype(jnp.float32)], axis=1)
    tall = lax.broadcasted_iota(jnp.int32, (RANK, 2 * RANK), 0)
    for k in range(RANK - 1):
        pivot = work[k : k + 1, :]
        scale = work[:, k : k + 1] / pivot[:, k : k + 1]
        work = jnp.where(tall > k, work - scale * pivot, work)
    inverse = work[:, RANK:]
    diagonal = jnp.sum(jnp.where(row == col, work[:, :RANK], 0.0), axis=1, keepdims=True)
    basis = dot_exact(inverse, left_ref[...])
    scaled = dot_exact(basis, inverse / diagonal, first_dims)
    high, low = kernel_split(scaled, 2)
    out_ref[...] = jnp.concatenate([high, high, low], axis=1)


def whiten(chunks, left):
    rows = left.shape[1]
    width = LANES * peers_of(X)
    last = chunks.shape[2] // width - 1
    return pl.pallas_call(
        whiten_kernel,
        grid=(1,),
        in_specs=[
            pl.BlockSpec((*chunks.shape[:2], width), lambda i: (0, 0, last)),
            pl.BlockSpec(left.shape, lambda i: (0, 0)),
        ],
        out_specs=pl.BlockSpec((rows, 3 * RANK), lambda i: (0, 0)),
        out_shape=jax.ShapeDtypeStruct((rows, 3 * RANK), jnp.bfloat16),
        compiler_params=params(16),
        cost_estimate=cost(400_000_000, 4_000_000),
    )(chunks, left)


def update_kernel(scaled_ref, right_ref, out_ref, held, sems):
    block = 512
    copies = []
    for i in range(held.shape[1] // block):
        place = slice(i * block, (i + 1) * block)
        high, low = kernel_split(right_ref[:, :, :, place].reshape(RANK, block), 2)
        terms = jnp.concatenate([high, low, high], axis=0)
        held[:, place] = dot32(scaled_ref[...], terms).astype(jnp.bfloat16)
        place = pl.ds(i * block, block)
        copies.append(pltpu.make_async_copy(held.at[:, place], out_ref.at[:, place], sems.at[i]))
        copies[-1].start()
    for copy in copies:
        copy.wait()


def update_product(scaled, right):
    rows, cols = scaled.shape[0], right.shape[-1]
    return pl.pallas_call(
        update_kernel,
        in_specs=[WHOLE] * 2,
        out_specs=pl.BlockSpec(memory_space=pl.ANY),
        out_shape=jax.ShapeDtypeStruct((rows, cols), jnp.bfloat16),
        scratch_shapes=[
            pltpu.VMEM((rows, cols), jnp.bfloat16),
            pltpu.SemaphoreType.DMA((cols // 512,)),
        ],
        compiler_params=params(16),
        cost_estimate=cost(6 * rows * cols * RANK, 2 * cols * rows),
    )(scaled, right)


def copies_kernel(chunks_ref, out_ref):
    total = chunks_ref[0]
    for peer in range(1, chunks_ref.shape[0]):
        total = total + chunks_ref[peer]
    for peer in range(out_ref.shape[0]):
        out_ref[peer] = total


def sum_copies(chunks, axes, cols):
    sources, rows, _ = chunks.shape
    shape = (peers_of(axes), rows, cols)
    return pl.pallas_call(
        copies_kernel,
        grid=(1,),
        in_specs=[pl.BlockSpec((sources, rows, cols), lambda i: (0, 0, 0))],
        out_specs=pl.BlockSpec(shape, lambda i: (0, 0, 0)),
        out_shape=pltpu.VMEM(shape, jnp.float32),
        compiler_params=params(8),
        cost_estimate=cost(sources * rows * cols, 4 * sources * rows * cols),
    )(chunks)


def exchange(chunks, axes):
    return lax.all_to_all(chunks, axes, 0, 0)


def after(first, *values):
    return lax.optimization_barrier((first, *values))


def local(activations, out_grads, residue, warm_start):
    residue = residue[0]
    rows, cols = residue.shape
    is_first = lax.axis_index("core") == 0
    left, *held = left_product(activations, out_grads, residue, warm_start)
    left, is_first = after(left, is_first)
    left = sum_copies(exchange(left.reshape(peers_of(LEFT_NEAR), -1, rows), LEFT_NEAR), LEFT_FAR, rows)
    left = sum_copies(exchange(left, LEFT_FAR), LEFT_NEAR, rows)
    left = exchange(left, LEFT_NEAR).reshape(RANK, rows)

    kept, sent = right_product(left, *held)
    sent = lax.all_gather(sent, "core", axis=0)
    chunks = exchange(kept + jnp.where(is_first, sent[1], sent[0]), NEAR_X)
    scaled = whiten(chunks, left)
    right = exchange(sum_copies(chunks, FAR, cols), FAR)
    right, scaled = after(sum_copies(right, NEAR_X, cols), scaled)
    right = lax.all_gather(exchange(right, NEAR_X), "core", axis=0)
    return update_product(scaled, right)


def solution(mesh):
    fine = Mesh(mesh.devices.reshape(*GRID.values()), tuple(GRID))
    in_specs = (P(DP, TENSOR), P(DP, None), P(DP, TENSOR, None), P())
    return jax.shard_map(local, mesh=fine, in_specs=in_specs, out_specs=P(TENSOR, None), check_vma=False)
```

```python
import math

import jax
import jax.numpy as jnp
from jax import lax
from jax.experimental import pallas as pl
from jax.experimental.pallas import tpu as pltpu
from jax.sharding import Mesh, PartitionSpec as P

RANK = 64
HALF = RANK // 2
LANES = 2 * RANK
GRAD_BLOCKS = 2
GRID = {"yA": 2, "yB": 2, "yC": 2, "zA": 2, "zB": 2, "zC": 2, "xA": 2, "xB": 2, "core": 2}
DP = ("yA", "yB", "yC", "zA", "zB", "zC")
TENSOR = ("xA", "xB", "core")
LEFT_NEAR, LEFT_FAR = ("zC", "zB", "zA"), ("yC", "yB", "yA")
NEAR = ("zC", "yC")
X = ("xB", "xA")
NEAR_X = (*X, "zC", "yC")
FAR = ("zB", "zA", "yA", "yB")

highest_precision = lax.Precision.HIGHEST
plain_dims = (((1,), (0,)), ((), ()))
first_dims = (((0,), (0,)), ((), ()))
last_dims = (((1,), (1,)), ((), ()))


def dot32(left, right, dims=plain_dims):
    return lax.dot_general(left, right, dims, preferred_element_type=jnp.float32)


def dot_exact(left, right, dims=plain_dims):
    return lax.dot_general(
        left, right, dims, precision=highest_precision, preferred_element_type=jnp.float32
    )


def split(value, terms):
    parts = []
    for _ in range(terms):
        part = lax.reduce_precision(value, 8, 7)
        parts.append(part.astype(jnp.bfloat16))
        value = value - part
    return parts


def kernel_split(value, terms):
    parts = []
    for _ in range(terms):
        part = value.astype(jnp.bfloat16)
        parts.append(part)
        value = value - part.astype(jnp.float32)
    return parts


def peers_of(axes):
    return math.prod(GRID[axis] for axis in axes)


def params(megabytes):
    return pltpu.CompilerParams(vmem_limit_bytes=megabytes * 1024 * 1024)


def cost(flops, moved):
    return pl.CostEstimate(flops=flops, bytes_accessed=moved, transcendentals=0)


WHOLE = pl.BlockSpec(memory_space=pltpu.VMEM)


def left_kernel(act_hbm, grad_hbm, res_hbm, warm_hbm, out_ref, act_ref, grad_ref, res_ref, warm_ref, sems):
    tokens = grad_ref.shape[0]
    block = tokens // GRAD_BLOCKS
    places = [pl.ds(i * block, block) for i in range(GRAD_BLOCKS)]
    moves = [(warm_hbm, warm_ref), (res_hbm, res_ref)]
    moves += [(grad_hbm.at[place], grad_ref.at[place]) for place in places]
    moves += [(act_hbm, act_ref)]
    copies = [pltpu.make_async_copy(*move, sems.at[i]) for i, move in enumerate(moves)]
    for copy in copies:
        copy.start()
    copies[0].wait()
    warm = warm_ref[...]
    copies[1].wait()
    left = dot32(warm, res_ref[...], last_dims)
    projected = []
    for i, place in enumerate(places):
        copies[2 + i].wait()
        terms = kernel_split(dot32(warm, grad_ref[place, :], last_dims), 3)
        projected.append(jnp.concatenate(terms, axis=0))
    copies[-1].wait()
    terms = dot32(jnp.concatenate(projected, axis=1), act_ref[...])
    out_ref[...] = terms[:RANK] + (terms[RANK : 2 * RANK] + terms[2 * RANK :]) + left


def left_product(activations, out_grads, residue, warm_start):
    tokens, rows = activations.shape
    cols = out_grads.shape[1]
    arrays = [activations, out_grads, residue, warm_start.T]
    held = [pltpu.VMEM(array.shape, array.dtype) for array in arrays[:3]]
    return pl.pallas_call(
        left_kernel,
        in_specs=[pl.BlockSpec(memory_space=pltpu.HBM)] * 4,
        out_specs=[WHOLE] * 4,
        out_shape=[pltpu.VMEM((RANK, rows), jnp.float32), *held],
        scratch_shapes=[
            pltpu.VMEM((RANK, cols), warm_start.dtype),
            pltpu.SemaphoreType.DMA((3 + GRAD_BLOCKS,)),
        ],
        compiler_params=params(16),
        cost_estimate=cost(2 * tokens * cols * RANK, 2 * cols * (tokens + rows)),
    )(*[pltpu.with_memory_space_constraint(array, pltpu.HBM) for array in arrays])


def right_kernel(left_ref, act_ref, grad_ref, res_ref, kept_ref, sent_ref):
    cols = grad_ref.shape[1]
    peers, pair, _ = kept_ref.shape
    left = left_ref[...]
    swapped = jnp.concatenate([left[HALF:], left[:HALF]], axis=0)
    ordered = kernel_split(jnp.where(lax.axis_index("core") == 0, left, swapped), 2)
    ordered = jnp.concatenate(ordered, axis=0)
    inner = dot32(ordered, act_ref[...], last_dims)
    inner = jnp.concatenate(kernel_split(inner[:RANK] + inner[RANK:], 2), axis=0)
    block = 512
    for start in range(0, cols, block):
        place = slice(start, start + block)
        terms = dot32(inner, grad_ref[:, place]) + dot32(ordered, res_ref[:, place])
        product = terms[:RANK] + terms[RANK:]
        kept_ref[:, :, place] = product[:HALF].reshape(peers, pair, block)
        sent_ref[:, :, place] = product[HALF:].reshape(peers, pair, block)

    gram = dot_exact(left, left, last_dims)
    gram = jnp.concatenate([gram[:HALF], gram[HALF:]], axis=1)
    shares = peers_of(NEAR)
    height = HALF // shares
    share = gram[:height]
    mine = lax.axis_index(NEAR)
    for other in range(1, shares):
        share = jnp.where(mine == other, gram[other * height : (other + 1) * height], share)
    for i in range(height // pair):
        place = slice(cols + i * LANES, cols + (i + 1) * LANES)
        piece = jnp.broadcast_to(share[i * pair : (i + 1) * pair][None], (peers, pair, LANES))
        kept_ref[:, :, place] = piece
        sent_ref[:, :, place] = piece


def right_product(left, activations, out_grads, residue):
    (rows, cols), tokens = residue.shape, out_grads.shape[0]
    peers = peers_of(NEAR_X)
    shape = (peers, HALF // peers, cols + LANES * peers_of(X))
    return pl.pallas_call(
        right_kernel,
        in_specs=[WHOLE] * 4,
        out_specs=[WHOLE] * 2,
        out_shape=[jax.ShapeDtypeStruct(shape, jnp.float32)] * 2,
        compiler_params=params(16),
        cost_estimate=cost(4 * (tokens + rows) * cols * RANK, 2 * cols * (tokens + rows)),
    )(left, activations, out_grads, residue)


def whiten_kernel(gram_ref, left_ref, out_ref):
    shares, sources, pair = peers_of(NEAR), peers_of(X), gram_ref.shape[1]
    pieces = []
    for share in range(shares):
        for i in range(HALF // shares // pair):
            place = slice(i * LANES, (i + 1) * LANES)
            piece = gram_ref[share, :, place]
            for source in range(1, sources):
                piece = piece + gram_ref[source * shares + share, :, place]
            pieces.append(piece)
    gram = jnp.concatenate(pieces, axis=0)
    gram = jnp.concatenate([gram[:, :RANK], gram[:, RANK:]], axis=0)
    row = lax.broadcasted_iota(jnp.int32, (RANK, RANK), 0)
    col = lax.broadcasted_iota(jnp.int32, (RANK, RANK), 1)
    work = jnp.concatenate([gram, (row == col).astype(jnp.float32)], axis=1)
    tall = lax.broadcasted_iota(jnp.int32, (RANK, 2 * RANK), 0)
    weighted = []
    for k in range(0, RANK, 2):
        first, second = work[k : k + 1, :], work[k + 1 : k + 2, :]
        corner, beside = 1.0 / first[:, k : k + 1], first[:, k + 1 : k + 2]
        ratio = beside * corner
        rest = 1.0 / (second[:, k + 1 : k + 2] - ratio * beside)
        second = (second - ratio * first) * rest
        first = (first - beside * second) * corner
        weighted += [first[:, RANK:], second[:, RANK:]]
        if k + 2 < RANK:
            step = work[:, k : k + 1] * first + work[:, k + 1 : k + 2] * second
            work = jnp.where(tall > k + 1, work - step, work)
    basis = dot_exact(work[:, RANK:], left_ref[...])
    scaled = dot_exact(basis, jnp.concatenate(weighted, axis=0), first_dims)
    high, low = kernel_split(scaled, 2)
    out_ref[...] = jnp.concatenate([high, high, low], axis=1)


def whiten(chunks, left):
    rows = left.shape[1]
    width = LANES * peers_of(X)
    last = chunks.shape[2] // width - 1
    return pl.pallas_call(
        whiten_kernel,
        grid=(1,),
        in_specs=[
            pl.BlockSpec((*chunks.shape[:2], width), lambda i: (0, 0, last)),
            pl.BlockSpec(left.shape, lambda i: (0, 0)),
        ],
        out_specs=pl.BlockSpec((rows, 3 * RANK), lambda i: (0, 0)),
        out_shape=jax.ShapeDtypeStruct((rows, 3 * RANK), jnp.bfloat16),
        compiler_params=params(16),
        cost_estimate=cost(400_000_000, 4_000_000),
    )(chunks, left)


def update_kernel(scaled_ref, right_ref, out_ref, held, sems):
    block = 512
    copies = []
    for i in range(held.shape[1] // block):
        place = slice(i * block, (i + 1) * block)
        high, low = kernel_split(right_ref[:, :, :, place].reshape(RANK, block), 2)
        terms = jnp.concatenate([high, low, high], axis=0)
        held[:, place] = dot32(scaled_ref[...], terms).astype(jnp.bfloat16)
        place = pl.ds(i * block, block)
        copies.append(pltpu.make_async_copy(held.at[:, place], out_ref.at[:, place], sems.at[i]))
        copies[-1].start()
    for copy in copies:
        copy.wait()


def update_product(scaled, right):
    rows, cols = scaled.shape[0], right.shape[-1]
    return pl.pallas_call(
        update_kernel,
        in_specs=[WHOLE] * 2,
        out_specs=pl.BlockSpec(memory_space=pl.ANY),
        out_shape=jax.ShapeDtypeStruct((rows, cols), jnp.bfloat16),
        scratch_shapes=[
            pltpu.VMEM((rows, cols), jnp.bfloat16),
            pltpu.SemaphoreType.DMA((cols // 512,)),
        ],
        compiler_params=params(16),
        cost_estimate=cost(6 * rows * cols * RANK, 2 * cols * rows),
    )(scaled, right)


def copies_kernel(chunks_ref, out_ref):
    total = chunks_ref[0]
    for peer in range(1, chunks_ref.shape[0]):
        total = total + chunks_ref[peer]
    for peer in range(out_ref.shape[0]):
        out_ref[peer] = total


def sum_copies(chunks, axes, cols):
    sources, rows, _ = chunks.shape
    shape = (peers_of(axes), rows, cols)
    return pl.pallas_call(
        copies_kernel,
        grid=(1,),
        in_specs=[pl.BlockSpec((sources, rows, cols), lambda i: (0, 0, 0))],
        out_specs=pl.BlockSpec(shape, lambda i: (0, 0, 0)),
        out_shape=pltpu.VMEM(shape, jnp.float32),
        compiler_params=params(8),
        cost_estimate=cost(sources * rows * cols, 4 * sources * rows * cols),
    )(chunks)


def exchange(chunks, axes):
    return lax.all_to_all(chunks, axes, 0, 0)


def after(first, *values):
    return lax.optimization_barrier((first, *values))


def local(activations, out_grads, residue, warm_start):
    residue = residue[0]
    rows, cols = residue.shape
    is_first = lax.axis_index("core") == 0
    left, *held = left_product(activations, out_grads, residue, warm_start)
    left, is_first = after(left, is_first)
    left = sum_copies(exchange(left.reshape(peers_of(LEFT_NEAR), -1, rows), LEFT_NEAR), LEFT_FAR, rows)
    left = sum_copies(exchange(left, LEFT_FAR), LEFT_NEAR, rows)
    left = exchange(left, LEFT_NEAR).reshape(RANK, rows)

    kept, sent = right_product(left, *held)
    sent = lax.all_gather(sent, "core", axis=0)
    chunks = exchange(kept + jnp.where(is_first, sent[1], sent[0]), NEAR_X)
    right = exchange(sum_copies(chunks, FAR, cols), FAR)
    right, chunks = after(sum_copies(right, NEAR_X, cols), chunks)
    scaled = whiten(chunks, left)
    right = lax.all_gather(exchange(right, NEAR_X), "core", axis=0)
    return update_product(scaled, right)


def solution(mesh):
    fine = Mesh(mesh.devices.reshape(*GRID.values()), tuple(GRID))
    in_specs = (P(DP, TENSOR), P(DP, None), P(DP, TENSOR, None), P())
    return jax.shard_map(local, mesh=fine, in_specs=in_specs, out_specs=P(TENSOR, None), check_vma=False)
```

```python
import math

import jax
import jax.numpy as jnp
from jax import lax
from jax.experimental import pallas as pl
from jax.experimental.pallas import tpu as pltpu
from jax.sharding import Mesh, PartitionSpec as P

RANK = 64
HALF = RANK // 2
LANES = 2 * RANK
GRAD_BLOCKS = 2
GRID = {"yA": 2, "yB": 2, "yC": 2, "zA": 2, "zB": 2, "zC": 2, "xA": 2, "xB": 2, "core": 2}
DP = ("yA", "yB", "yC", "zA", "zB", "zC")
TENSOR = ("xA", "xB", "core")
LEFT_NEAR, LEFT_FAR = ("zB", "zC", "zA"), ("yB", "yC", "yA")
NEAR = ("zC", "yC")
X = ("xB", "xA")
NEAR_X = (*X, "zC", "yC")
FAR = ("yB", "yA", "zA", "zB")

highest_precision = lax.Precision.HIGHEST
plain_dims = (((1,), (0,)), ((), ()))
first_dims = (((0,), (0,)), ((), ()))
last_dims = (((1,), (1,)), ((), ()))


def dot32(left, right, dims=plain_dims):
    return lax.dot_general(left, right, dims, preferred_element_type=jnp.float32)


def dot_exact(left, right, dims=plain_dims):
    return lax.dot_general(
        left, right, dims, precision=highest_precision, preferred_element_type=jnp.float32
    )


def split(value, terms):
    parts = []
    for _ in range(terms):
        part = lax.reduce_precision(value, 8, 7)
        parts.append(part.astype(jnp.bfloat16))
        value = value - part
    return parts


def kernel_split(value, terms):
    parts = []
    for _ in range(terms):
        part = value.astype(jnp.bfloat16)
        parts.append(part)
        value = value - part.astype(jnp.float32)
    return parts


def peers_of(axes):
    return math.prod(GRID[axis] for axis in axes)


def params(megabytes):
    return pltpu.CompilerParams(vmem_limit_bytes=megabytes * 1024 * 1024)


def cost(flops, moved):
    return pl.CostEstimate(flops=flops, bytes_accessed=moved, transcendentals=0)


WHOLE = pl.BlockSpec(memory_space=pltpu.VMEM)


def left_kernel(act_hbm, grad_hbm, res_hbm, warm_hbm, out_ref, act_ref, grad_ref, res_ref, warm_ref, sems):
    tokens = grad_ref.shape[0]
    block = tokens // GRAD_BLOCKS
    places = [pl.ds(i * block, block) for i in range(GRAD_BLOCKS)]
    moves = [(warm_hbm, warm_ref), (res_hbm, res_ref)]
    moves += [(grad_hbm.at[place], grad_ref.at[place]) for place in places]
    moves += [(act_hbm, act_ref)]
    copies = [pltpu.make_async_copy(*move, sems.at[i]) for i, move in enumerate(moves)]
    for copy in copies:
        copy.start()
    copies[0].wait()
    warm = warm_ref[...]
    copies[1].wait()
    left = dot32(warm, res_ref[...], last_dims)
    projected = []
    for i, place in enumerate(places):
        copies[2 + i].wait()
        terms = kernel_split(dot32(warm, grad_ref[place, :], last_dims), 3)
        projected.append(jnp.concatenate(terms, axis=0))
    copies[-1].wait()
    terms = dot32(jnp.concatenate(projected, axis=1), act_ref[...])
    out_ref[...] = terms[:RANK] + (terms[RANK : 2 * RANK] + terms[2 * RANK :]) + left


def left_product(activations, out_grads, residue, warm_start):
    tokens, rows = activations.shape
    cols = out_grads.shape[1]
    arrays = [activations, out_grads, residue, warm_start.T]
    held = [pltpu.VMEM(array.shape, array.dtype) for array in arrays[:3]]
    return pl.pallas_call(
        left_kernel,
        in_specs=[pl.BlockSpec(memory_space=pltpu.HBM)] * 4,
        out_specs=[WHOLE] * 4,
        out_shape=[pltpu.VMEM((RANK, rows), jnp.float32), *held],
        scratch_shapes=[
            pltpu.VMEM((RANK, cols), warm_start.dtype),
            pltpu.SemaphoreType.DMA((3 + GRAD_BLOCKS,)),
        ],
        compiler_params=params(16),
        cost_estimate=cost(2 * tokens * cols * RANK, 2 * cols * (tokens + rows)),
    )(*[pltpu.with_memory_space_constraint(array, pltpu.HBM) for array in arrays])


def right_kernel(left_ref, act_ref, grad_ref, res_ref, kept_ref, sent_ref):
    cols = grad_ref.shape[1]
    peers, pair, _ = kept_ref.shape
    left = left_ref[...]
    swapped = jnp.concatenate([left[HALF:], left[:HALF]], axis=0)
    ordered = kernel_split(jnp.where(lax.axis_index("core") == 0, left, swapped), 2)
    ordered = jnp.concatenate(ordered, axis=0)
    inner = dot32(ordered, act_ref[...], last_dims)
    inner = jnp.concatenate(kernel_split(inner[:RANK] + inner[RANK:], 2), axis=0)
    block = 512
    for start in range(0, cols, block):
        place = slice(start, start + block)
        terms = dot32(inner, grad_ref[:, place]) + dot32(ordered, res_ref[:, place])
        product = terms[:RANK] + terms[RANK:]
        kept_ref[:, :, place] = product[:HALF].reshape(peers, pair, block)
        sent_ref[:, :, place] = product[HALF:].reshape(peers, pair, block)

    gram = dot_exact(left, left, last_dims)
    gram = jnp.concatenate([gram[:HALF], gram[HALF:]], axis=1)
    shares = peers_of(NEAR)
    height = HALF // shares
    share = gram[:height]
    mine = lax.axis_index(NEAR)
    for other in range(1, shares):
        share = jnp.where(mine == other, gram[other * height : (other + 1) * height], share)
    for i in range(height // pair):
        place = slice(cols + i * LANES, cols + (i + 1) * LANES)
        piece = jnp.broadcast_to(share[i * pair : (i + 1) * pair][None], (peers, pair, LANES))
        kept_ref[:, :, place] = piece
        sent_ref[:, :, place] = piece


def right_product(left, activations, out_grads, residue):
    (rows, cols), tokens = residue.shape, out_grads.shape[0]
    peers = peers_of(NEAR_X)
    shape = (peers, HALF // peers, cols + LANES * peers_of(X))
    return pl.pallas_call(
        right_kernel,
        in_specs=[WHOLE] * 4,
        out_specs=[WHOLE] * 2,
        out_shape=[jax.ShapeDtypeStruct(shape, jnp.float32)] * 2,
        compiler_params=params(16),
        cost_estimate=cost(4 * (tokens + rows) * cols * RANK, 2 * cols * (tokens + rows)),
    )(left, activations, out_grads, residue)


def whiten_kernel(gram_ref, left_ref, out_ref):
    shares, sources, pair = peers_of(NEAR), peers_of(X), gram_ref.shape[1]
    pieces = []
    for share in range(shares):
        for i in range(HALF // shares // pair):
            place = slice(i * LANES, (i + 1) * LANES)
            piece = gram_ref[share, :, place]
            for source in range(1, sources):
                piece = piece + gram_ref[source * shares + share, :, place]
            pieces.append(piece)
    gram = jnp.concatenate(pieces, axis=0)
    gram = jnp.concatenate([gram[:, :RANK], gram[:, RANK:]], axis=0)
    row = lax.broadcasted_iota(jnp.int32, (RANK, RANK), 0)
    col = lax.broadcasted_iota(jnp.int32, (RANK, RANK), 1)
    work = jnp.concatenate([gram, (row == col).astype(jnp.float32)], axis=1)
    tall = lax.broadcasted_iota(jnp.int32, (RANK, 2 * RANK), 0)
    for k in range(RANK - 1):
        pivot = work[k : k + 1, :]
        scale = work[:, k : k + 1] / pivot[:, k : k + 1]
        work = jnp.where(tall > k, work - scale * pivot, work)
    inverse = work[:, RANK:]
    diagonal = jnp.sum(jnp.where(row == col, work[:, :RANK], 0.0), axis=1, keepdims=True)
    basis = dot_exact(inverse, left_ref[...])
    scaled = dot_exact(basis, inverse / diagonal, first_dims)
    high, low = kernel_split(scaled, 2)
    out_ref[...] = jnp.concatenate([high, high, low], axis=1)


def whiten(chunks, left):
    rows = left.shape[1]
    width = LANES * peers_of(X)
    last = chunks.shape[2] // width - 1
    return pl.pallas_call(
        whiten_kernel,
        grid=(1,),
        in_specs=[
            pl.BlockSpec((*chunks.shape[:2], width), lambda i: (0, 0, last)),
            pl.BlockSpec(left.shape, lambda i: (0, 0)),
        ],
        out_specs=pl.BlockSpec((rows, 3 * RANK), lambda i: (0, 0)),
        out_shape=jax.ShapeDtypeStruct((rows, 3 * RANK), jnp.bfloat16),
        compiler_params=params(16),
        cost_estimate=cost(400_000_000, 4_000_000),
    )(chunks, left)


def update_kernel(scaled_ref, right_ref, out_ref, held, sems):
    block = 512
    copies = []
    for i in range(held.shape[1] // block):
        place = slice(i * block, (i + 1) * block)
        high, low = kernel_split(right_ref[:, :, :, place].reshape(RANK, block), 2)
        terms = jnp.concatenate([high, low, high], axis=0)
        held[:, place] = dot32(scaled_ref[...], terms).astype(jnp.bfloat16)
        place = pl.ds(i * block, block)
        copies.append(pltpu.make_async_copy(held.at[:, place], out_ref.at[:, place], sems.at[i]))
        copies[-1].start()
    for copy in copies:
        copy.wait()


def update_product(scaled, right):
    rows, cols = scaled.shape[0], right.shape[-1]
    return pl.pallas_call(
        update_kernel,
        in_specs=[WHOLE] * 2,
        out_specs=pl.BlockSpec(memory_space=pl.ANY),
        out_shape=jax.ShapeDtypeStruct((rows, cols), jnp.bfloat16),
        scratch_shapes=[
            pltpu.VMEM((rows, cols), jnp.bfloat16),
            pltpu.SemaphoreType.DMA((cols // 512,)),
        ],
        compiler_params=params(16),
        cost_estimate=cost(6 * rows * cols * RANK, 2 * cols * rows),
    )(scaled, right)


def copies_kernel(chunks_ref, out_ref):
    total = chunks_ref[0]
    for peer in range(1, chunks_ref.shape[0]):
        total = total + chunks_ref[peer]
    for peer in range(out_ref.shape[0]):
        out_ref[peer] = total


def sum_copies(chunks, axes, cols):
    sources, rows, _ = chunks.shape
    shape = (peers_of(axes), rows, cols)
    return pl.pallas_call(
        copies_kernel,
        grid=(1,),
        in_specs=[pl.BlockSpec((sources, rows, cols), lambda i: (0, 0, 0))],
        out_specs=pl.BlockSpec(shape, lambda i: (0, 0, 0)),
        out_shape=pltpu.VMEM(shape, jnp.float32),
        compiler_params=params(8),
        cost_estimate=cost(sources * rows * cols, 4 * sources * rows * cols),
    )(chunks)


def exchange(chunks, axes):
    return lax.all_to_all(chunks, axes, 0, 0)


def after(first, *values):
    return lax.optimization_barrier((first, *values))


def local(activations, out_grads, residue, warm_start):
    residue = residue[0]
    rows, cols = residue.shape
    is_first = lax.axis_index("core") == 0
    left, *held = left_product(activations, out_grads, residue, warm_start)
    left, is_first = after(left, is_first)
    left = sum_copies(exchange(left.reshape(peers_of(LEFT_NEAR), -1, rows), LEFT_NEAR), LEFT_FAR, rows)
    left = sum_copies(exchange(left, LEFT_FAR), LEFT_NEAR, rows)
    left = exchange(left, LEFT_NEAR).reshape(RANK, rows)

    kept, sent = right_product(left, *held)
    sent = lax.all_gather(sent, "core", axis=0)
    chunks = exchange(kept + jnp.where(is_first, sent[1], sent[0]), NEAR_X)
    right = exchange(sum_copies(chunks, FAR, cols), FAR)
    right, chunks = after(sum_copies(right, NEAR_X, cols), chunks)
    scaled = whiten(chunks, left)
    right = lax.all_gather(exchange(right, NEAR_X), "core", axis=0)
    return update_product(scaled, right)


def solution(mesh):
    fine = Mesh(mesh.devices.reshape(*GRID.values()), tuple(GRID))
    in_specs = (P(DP, TENSOR), P(DP, None), P(DP, TENSOR, None), P())
    return jax.shard_map(local, mesh=fine, in_specs=in_specs, out_specs=P(TENSOR, None), check_vma=False)
```
